256 devices in a mesh: group: 8 (over z), ctx: 4 (over x_lo, core), head: 8 (over y, x_hi).
Axes of the slice: x: 4 (x_hi: 2, x_lo: 2; x = x_hi * 2 + x_lo), y: 4, z: 8, core: 2. Of those that a mesh axis runs over, the one named last changes fastest.
Arguments:
- prompt_q: bfloat16 [4096, 8192], P(('group', 'ctx'), 'head'), may hold values from -120 to 120
- prompt_kv: bfloat16 [2, 4096, 1024], P(None, ('group', 'ctx'), 'head'), may hold values from -4 to 4
- cont_q: bfloat16 [32, 256, 8192], P(('group', 'ctx'), None, 'head'), may hold values from -120 to 120
- cont_kv: bfloat16 [2, 32, 256, 1024], P(None, ('group', 'ctx'), None, 'head'), may hold values from -4 to 4
- cont_len: int32 [32], P(('group', 'ctx')), may hold values from 1 to 256, 4096 in all
Outputs:
- prompt_out: bfloat16 [4096, 8192], P(('group', 'ctx', 'head'))
- cont_out: bfloat16 [32, 256, 8192], P(('group', 'ctx'), 'head')
The draws below stay inside these ranges and needn't reach their ends.
Inputs may be any that keep to these rules, and one draw needn't show every extreme that they name: The live positions of continuation c are its first cont_len[c] slots.
All inputs are finite; a program needn't handle non-finite values. No bound on the sum of `cont_len` on one device may be relied on, other than what follows from the above.
Results may differ from the reference program's by a relative error of at most 0.009.
Values may be sent and summed in bfloat16 or wider, within the bound.
No kernel may reach another device: no remote copies, remote signals or barrier semaphores. Data moves between devices by JAX's collectives and lax.ppermute only.
A program may use at most 128 MiB of HBM per device.

```python
import math
import jax
import jax.numpy as jnp
import numpy as np
from jax import lax

QH = 64
KVH = 8
HD = 128
GQA = 8
LEN = 256
PROMPT = 4096
CONTS = 32


def drawn_key_rows(key):
    key = jax.random.fold_in(key, 50)
    return jnp.clip(jax.random.normal(key, (PROMPT, KVH * HD), jnp.float32), -4.0, 4.0)


def draw_prompt_kv(key, part):
    key_rows = drawn_key_rows(key)
    key = jax.random.fold_in(key, 1)
    values = jnp.clip(jax.random.normal(key, (PROMPT, KVH * HD), jnp.float32), -4.0, 4.0)
    return jnp.stack([key_rows, values]).astype(jnp.bfloat16)


def draw_prompt_q(key, part):
    key = jax.random.fold_in(key, 2)
    normal_part = jnp.clip(jax.random.normal(key, (PROMPT, QH * HD), jnp.float32), -4.0, 4.0)
    return normal_part.astype(jnp.bfloat16)


def draw_cont_q(key, part):
    key = jax.random.fold_in(key, 4)
    normal_part = jnp.clip(jax.random.normal(key, (CONTS, LEN, QH * HD), jnp.float32), -4.0, 4.0)
    return normal_part.astype(jnp.bfloat16)


def shard_levels(stream_key, extent, cuts, low, largest):
    def one(position, parts):
        heights = jax.random.uniform(jax.random.fold_in(jax.random.fold_in(stream_key, 6), position), (parts,), jnp.float32, low / len(cuts), largest / len(cuts))
        return jnp.repeat(jnp.exp(heights), extent[position] // parts).reshape((-1,) + (1,) * (len(extent) - position - 1))

    factor_of = one(*cuts[0])
    for cut in cuts[1:]:
        factor_of = factor_of * one(*cut)
    return factor_of


def profile(amount, total, most, skew):
    portions = [(1 << 20) // math.isqrt(standing ** skew) + 1 for standing in range(2, amount + 1)]
    surplus, holding = total - most - (amount - 1), [1] * (amount - 1)
    while surplus > 0:
        candidates = [i for i in range(amount - 1) if holding[i] < most]
        mass, budget = sum([portions[i] for i in candidates]), surplus
        for i in candidates:
            extra = min(most - holding[i], max(1, budget * portions[i] // mass), surplus)
            holding[i] = holding[i] + extra
            surplus = surplus - extra
    return np.array([most] + holding)


def ragged(stream_key, amount, total, bound, lean):
    if amount == 2:
        one = jax.random.randint(stream_key, (), max(1, total - bound), min(bound, total - 1) + 1)
        return jnp.stack([one, total - one])
    tallies = jnp.asarray(profile(amount, total, bound, lean), jnp.int32)
    pairs = (amount - 1) // 2
    donor, sink = tallies[1:1 + 2 * pairs:2], tallies[2:2 + 2 * pairs:2]
    room = jnp.minimum(donor - 1, bound - sink)
    passed = jax.random.randint(jax.random.fold_in(stream_key, 1), (pairs,), 0, 1 << 20) % (room + 1)
    tallies = tallies.at[1:1 + 2 * pairs:2].set(donor - passed).at[2:2 + 2 * pairs:2].set(sink + passed)
    return tallies[jax.random.permutation(jax.random.fold_in(stream_key, 2), amount)]


def bell_draw(own_key, extent, width, limit, cuts=(), kind=jnp.bfloat16):
    factor_of = shard_levels(own_key, extent, cuts, -0.22, 0.18) if cuts else 1.0
    array = jax.random.normal(own_key, extent, jnp.float32) * width * factor_of
    return jnp.minimum(jnp.maximum(array, -limit), limit).astype(kind)


def setup_inputs(seed: int = 0) -> dict:
    keys = jax.random.split(jax.random.key(seed), 6)
    return {
        "prompt_q": draw_prompt_q(jax.random.fold_in(keys[5], 71), 0),
        "prompt_kv": draw_prompt_kv(jax.random.fold_in(keys[5], 71), 0),
        "cont_q": draw_cont_q(jax.random.fold_in(keys[5], 71), 0),
        "cont_kv": bell_draw(keys[3], (2, CONTS, LEN, KVH * HD), 1.0, 4.0, ((1, 32), (3, 8))),
        "cont_len": ragged(keys[4], CONTS, CONTS * LEN // 2, LEN, 2).astype(jnp.int32),
    }


def softmax_attend(queries, key_rows, value_rows, visible):
    scores = jnp.einsum('qgd,nd->gqn', queries.astype(jnp.float32), key_rows.astype(jnp.float32)) * HD ** -0.5
    scores = jnp.where(visible[None], scores, -jnp.inf)
    highest = jnp.max(scores, axis=-1, keepdims=True)
    raised = jnp.exp(scores - highest)
    denominator = jnp.sum(raised, axis=-1)
    weights = raised.astype(jnp.bfloat16)
    mixed = jnp.einsum('gqn,nd->qgd', weights.astype(jnp.float32), value_rows.astype(jnp.float32))
    return mixed / denominator.T[:, :, None]


def reference(prompt_q, prompt_kv, cont_q, cont_kv, cont_len):
    prompt_heads = prompt_q.reshape(PROMPT, KVH, GQA, HD).transpose(1, 0, 2, 3)
    prompt_keys = prompt_kv[0].reshape(PROMPT, KVH, HD).transpose(1, 0, 2)
    prompt_values = prompt_kv[1].reshape(PROMPT, KVH, HD).transpose(1, 0, 2)
    positions = jnp.arange(PROMPT, dtype=jnp.int32)
    causal = positions[None, :] <= positions[:, None]

    def prompt_head(inputs):
        queries, key_rows, value_rows = inputs
        return softmax_attend(queries, key_rows, value_rows, causal)

    prompt_mixed = lax.map(prompt_head, (prompt_heads, prompt_keys, prompt_values))
    prompt_out = prompt_mixed.transpose(1, 0, 2, 3).reshape(PROMPT, QH * HD).astype(jnp.bfloat16)

    cont_heads = cont_q.reshape(CONTS, LEN, KVH, GQA, HD).transpose(2, 0, 1, 3, 4)
    own_keys = cont_kv[0].reshape(CONTS, LEN, KVH, HD).transpose(2, 0, 1, 3)
    own_values = cont_kv[1].reshape(CONTS, LEN, KVH, HD).transpose(2, 0, 1, 3)
    slot_ids = jnp.arange(LEN, dtype=jnp.int32)
    shared_visible = jnp.ones((LEN, PROMPT), jnp.bool_)

    def one_head(inputs):
        queries, key_rows, value_rows, shared_keys, shared_values = inputs

        def one_cont(cont_item):
            cont_queries, cont_keys, cont_values, live_count = cont_item
            own_visible = (slot_ids[None, :] <= slot_ids[:, None]) & (slot_ids[None, :] < live_count)
            visible = jnp.concatenate([shared_visible, own_visible], axis=1)
            all_keys = jnp.concatenate([shared_keys, cont_keys], axis=0)
            all_values = jnp.concatenate([shared_values, cont_values], axis=0)
            mixed = softmax_attend(cont_queries, all_keys, all_values, visible)
            live_rows = (slot_ids < live_count)[:, None, None]
            return jnp.where(live_rows, mixed, 0.0)

        return lax.map(one_cont, (queries, key_rows, value_rows, cont_len))

    cont_mixed = lax.map(one_head, (cont_heads, own_keys, own_values, prompt_keys, prompt_values))
    cont_out = cont_mixed.transpose(1, 2, 0, 3, 4).reshape(CONTS, LEN, QH * HD).astype(jnp.bfloat16)
    return prompt_out, cont_out
```

```python
import functools

import jax
import jax.numpy as jnp
from jax import lax
from jax.experimental import pallas as pl
from jax.experimental.pallas import tpu as pltpu
from jax.sharding import PartitionSpec as P

HD = 128
GQA = 8
ROWS_P = 128
ROWS_C = 256
ROWS = ROWS_P + ROWS_C
SLAB = 512
BLOCK = 128
LOW = -1e30
SCALE = HD**-0.5 * 1.4426950408889634

C_CORE = [(0, 1), (1, 0), (2, 3), (3, 2)]
C_X = [(0, 2), (2, 0), (1, 3), (3, 1)]
C_DIAG = [(0, 3), (3, 0), (1, 2), (2, 1)]


def update(q, keys, values, m, acc, mask=None):
    s = lax.dot_general(q, keys, (((1,), (1,)), ((), ())), preferred_element_type=jnp.float32)
    if mask is not None:
        s = jnp.where(mask, s, LOW)
    m_new = jnp.maximum(m, jnp.max(s, axis=1, keepdims=True))
    alpha = jnp.exp2((m - m_new) * SCALE)
    p = jnp.exp2(s * SCALE - m_new * SCALE).astype(jnp.bfloat16)
    acc = acc * alpha + jnp.dot(p, values, preferred_element_type=jnp.float32)
    return m_new, acc


def extend(vx, values):
    vx[:, :HD] = values
    vx[:, HD:] = jnp.ones((vx.shape[0], HD), jnp.bfloat16)


def own_kernel(meta, qc, kv, acc_out, m_out, vx):
    @pl.when(pl.program_id(0) == 0)
    def _():
        extend(vx, kv[1, 0])

    live = meta[0]
    keys = kv[0, 0]
    for r in range(0, ROWS_C, BLOCK):

        @pl.when(live > r)
        def _():
            row = r + lax.broadcasted_iota(jnp.int32, (BLOCK, ROWS_C), 0)
            col = lax.broadcasted_iota(jnp.int32, (BLOCK, ROWS_C), 1)
            m = jnp.full((BLOCK, 1), LOW, jnp.float32)
            acc = jnp.zeros((BLOCK, 2 * HD), jnp.float32)
            m, acc = update(qc[0, r : r + BLOCK, :], keys, vx[...], m, acc, (col <= row) & (col < live))
            at = pl.ds(ROWS_P + r, BLOCK)
            acc_out[0, at, :] = acc
            m_out[0, at, :] = jnp.broadcast_to(m, (BLOCK, HD))


def slab_kernel(n_slabs, step, last, *refs):
    own = step == 0
    meta, qp, qc = refs[:3]
    slabs = refs[3 : 3 + n_slabs]
    acc_in, m_in = refs[3 + n_slabs : 5 + n_slabs]
    rest = refs[5 + n_slabs :]
    vxs = rest[-n_slabs:]
    outs = rest[:-n_slabs]

    @pl.when(pl.program_id(0) == 0)
    def _():
        for vx, kv in zip(vxs, slabs):
            extend(vx, kv[1])

    live = meta[0]

    def load(at):
        return m_in[0, at, 0:1], acc_in[0, at, :]

    def store(at, m, acc):
        if last:
            mixed = acc[:, :HD] / acc[:, HD:]
            start = at.start
            if start < ROWS_P:
                outs[0][:, :16, :] = mixed.reshape(8, 16, HD).astype(jnp.bfloat16)
            else:
                r = start - ROWS_P
                row = r + lax.broadcasted_iota(jnp.int32, (BLOCK, HD), 0)
                mixed = jnp.where(row < live, mixed, 0.0).astype(jnp.bfloat16)
                outs[0][r // 32 : (r + BLOCK) // 32, 16:, :] = mixed.reshape(BLOCK // 32, 32, HD)
        else:
            outs[0][0, at, :] = acc
            outs[1][0, at, :] = jnp.broadcast_to(m, (BLOCK, HD))

    at = pl.ds(0, BLOCK)
    if own:
        ctx = meta[1]
        row = lax.broadcasted_iota(jnp.int32, (BLOCK, SLAB), 0) + ctx * BLOCK
        col = lax.broadcasted_iota(jnp.int32, (BLOCK, SLAB), 1)
        piece = col // BLOCK
        base = jnp.where(piece == 0, ctx, jnp.where(piece == 1, ctx ^ 1, jnp.where(piece == 2, ctx ^ 2, ctx ^ 3)))
        mask = base * BLOCK + (col % BLOCK) <= row
        m = jnp.full((BLOCK, 1), LOW, jnp.float32)
        acc = jnp.zeros((BLOCK, 2 * HD), jnp.float32)
        m, acc = update(qp[...], slabs[0][0], vxs[0][...], m, acc, mask)
        store(at, m, acc)
    else:
        ctx, z = meta[1], meta[2]
        way = 2 * (ctx & 1) - 1
        sees = [((z + (1 - 2 * i) * way * step) & 7) < z for i in range(n_slabs)]
        for code in range(2**n_slabs):
            bits = [(code >> i) & 1 for i in range(n_slabs)]
            cond = functools.reduce(
                jnp.logical_and, [s if b else jnp.logical_not(s) for s, b in zip(sees, bits)]
            )

            @pl.when(cond)
            def _():
                m, acc = load(at)
                for i in range(n_slabs):
                    if bits[i]:
                        m, acc = update(qp[...], slabs[i][0], vxs[i][...], m, acc)
                store(at, m, acc)

    for r in range(0, ROWS_C, BLOCK):
        at_c = pl.ds(ROWS_P + r, BLOCK)

        @pl.when(live > r)
        def _():
            m, acc = load(at_c)
            for kv, vx in zip(slabs, vxs):
                m, acc = update(qc[0, r : r + BLOCK, :], kv[0], vx[...], m, acc)
            store(at_c, m, acc)

        if last:

            @pl.when(live <= r)
            def _():
                outs[0][r // 32 : (r + BLOCK) // 32, 16:, :] = jnp.zeros((BLOCK // 32, 32, HD), jnp.bfloat16)


SMEM = pl.BlockSpec(memory_space=pltpu.SMEM)
QP = pl.BlockSpec((ROWS_P, HD), lambda h: (0, h))
QC = pl.BlockSpec((1, ROWS_C, HD), lambda h: (0, 0, h))
ACC = pl.BlockSpec((1, ROWS, 2 * HD), lambda h: (h, 0, 0))
MAX = pl.BlockSpec((1, ROWS, HD), lambda h: (h, 0, 0))
STATE = (
    jax.ShapeDtypeStruct((GQA, ROWS, 2 * HD), jnp.float32),
    jax.ShapeDtypeStruct((GQA, ROWS, HD), jnp.float32),
)
PARAMS = pltpu.CompilerParams(vmem_limit_bytes=40 << 20)


def cost(scores):
    return pl.CostEstimate(flops=scores * 512 * 2, bytes_accessed=1 << 20, transcendentals=scores)


def attend_own(meta, qc, kv):
    return pl.pallas_call(
        own_kernel,
        grid=(GQA,),
        in_specs=[SMEM, QC, pl.BlockSpec((2, 1, ROWS_C, HD), lambda h: (0, 0, 0, 0))],
        out_specs=(ACC, MAX),
        out_shape=STATE,
        scratch_shapes=[pltpu.VMEM((ROWS_C, 2 * HD), jnp.bfloat16)],
        compiler_params=PARAMS,
        cost_estimate=cost(GQA * ROWS_C * ROWS_C),
        name="own",
    )(meta, qc, kv)


def attend(meta, qp, qc, slabs, state, step, last=False):
    n = len(slabs)
    slab = pl.BlockSpec((2, SLAB, HD), lambda h: (0, 0, 0))
    if last:
        out_specs = pl.BlockSpec((8, 48, HD), lambda h: (0, 0, h))
        out_shape = jax.ShapeDtypeStruct((8, 48, GQA * HD), jnp.bfloat16)
        alias = {}
    else:
        out_specs, out_shape = (ACC, MAX), STATE
        alias = {3 + n: 0, 4 + n: 1}
    return pl.pallas_call(
        functools.partial(slab_kernel, n, step, last),
        grid=(GQA,),
        in_specs=[SMEM, QP, QC] + [slab] * n + [ACC, MAX],
        out_specs=out_specs,
        out_shape=out_shape,
        input_output_aliases=alias,
        scratch_shapes=[pltpu.VMEM((SLAB, 2 * HD), jnp.bfloat16)] * n,
        compiler_params=PARAMS,
        cost_estimate=cost(GQA * ROWS * SLAB * n),
        name=f"slabs{step % 5}_{n}",
    )(meta, qp, qc, *slabs, *state)


def tie(*trees):
    return lax.optimization_barrier(trees)


def body(prompt_q, prompt_kv, cont_q, cont_kv, cont_len):
    z = lax.axis_index("group")
    ctx = lax.axis_index("ctx")
    core = ctx % 2
    n_z = 8
    ring = [(g * 4 + c, ((g + (1 if c % 2 == 0 else -1)) % n_z) * 4 + c) for g in range(n_z) for c in range(4)]

    def pass_on(x):
        return lax.ppermute(x, ("group", "ctx"), ring)

    def swap(x):
        return lax.ppermute(x, "ctx", C_CORE)

    meta = jnp.stack([cont_len[0], ctx, z])
    pieces = [lax.ppermute(prompt_kv, "ctx", pairs) for pairs in (C_CORE, C_X, C_DIAG)]
    state = attend_own(meta, cont_q, cont_kv)
    pieces, state = tie(pieces, state)
    own = jnp.concatenate([prompt_kv] + pieces, axis=1)

    near = pass_on(own)
    state = attend(meta, prompt_q, cont_q, [own], state, 0)
    near, state = tie(near, state)

    other = swap(near)
    coming = pass_on(near)
    state = attend(meta, prompt_q, cont_q, [near], state, 1)
    other, state = tie(other, state)
    state = attend(meta, prompt_q, cont_q, [other], state, -1)
    near, state = tie(coming, state)

    for step in (2, 3):
        other = swap(near)
        coming = pass_on(near)
        state = attend(meta, prompt_q, cont_q, [near, other], state, step)
        near, state = tie(coming, state)
    mixed = attend(meta, prompt_q, cont_q, [near], state, 4, last=True)
    moved = lax.all_to_all(mixed, "head", split_axis=0, concat_axis=0, tiled=True)
    prompt_out = moved[:, :16].transpose(1, 0, 2).reshape(16, 8 * GQA * HD)
    cont_out = moved[:, 16:].transpose(1, 0, 2).reshape(1, 32, 8 * GQA * HD)
    return prompt_out, cont_out


def solution(mesh):
    placed = (
        P(("group", "ctx"), "head"),
        P(None, ("group", "ctx"), "head"),
        P(("group", "ctx"), None, "head"),
        P(None, ("group", "ctx"), None, "head"),
        P(("group", "ctx")),
    )
    return jax.shard_map(
        body,
        mesh=mesh,
        in_specs=placed,
        out_specs=(P(("group", "ctx", "head"), None), P(("group", "ctx"), "head", None)),
        check_vma=False,
    )
```

```python
import functools

import jax
import jax.numpy as jnp
from jax import lax
from jax.experimental import pallas as pl
from jax.experimental.pallas import tpu as pltpu
from jax.sharding import PartitionSpec as P

HD = 128
GQA = 8
ROWS_P = 128
ROWS_C = 256
ROWS = ROWS_P + ROWS_C
SLAB = 512
BLOCK = 128
LOW = -1e30
SCALE = HD**-0.5 * 1.4426950408889634

C_CORE = [(0, 1), (1, 0), (2, 3), (3, 2)]
C_X = [(0, 2), (2, 0), (1, 3), (3, 1)]
C_DIAG = [(0, 3), (3, 0), (1, 2), (2, 1)]


def update(q, keys, values, m, l, acc, mask=None):
    s = lax.dot_general(q, keys, (((1,), (1,)), ((), ())), preferred_element_type=jnp.float32)
    parts = [s[:, j : j + HD] for j in range(0, s.shape[1], HD)]
    if mask is not None:
        parts = [mask(j, part) for j, part in enumerate(parts)]
    top = functools.reduce(jnp.maximum, parts)
    m_new = jnp.maximum(m, jnp.max(top, axis=1, keepdims=True))
    alpha = jnp.exp2((m - m_new) * SCALE)
    shift = m_new * SCALE
    p = jnp.concatenate([jnp.exp2(part * SCALE - shift).astype(jnp.bfloat16) for part in parts], axis=1)
    pv = jnp.dot(p, values, preferred_element_type=jnp.float32)
    return m_new, l * alpha + pv[:, HD:], acc * alpha + pv[:, :HD]


def fresh():
    zero = jnp.zeros((BLOCK, HD), jnp.float32)
    return zero + LOW, zero, zero


def extend(vx, values):
    vx[:, :HD] = values
    vx[:, HD:] = jnp.ones((vx.shape[0], HD), jnp.bfloat16)


def over_heads(together, fn):
    if together == GQA:
        for h in range(GQA):
            fn(h)
        return

    def some(i, carry):
        for h in range(together):
            fn(i * together + h)
        return carry

    lax.fori_loop(0, GQA // together, some, 0)


def columns(h):
    return pl.ds(h * HD if isinstance(h, int) else pl.multiple_of(h * HD, HD), HD)


def own_kernel(meta, qc, kv, m_out, l_out, acc_out, vx):
    extend(vx, kv[1, 0])
    live = meta[0]

    def block(h, r):
        n = r + BLOCK

        def mask(j, part):
            row = r + lax.broadcasted_iota(jnp.int32, (BLOCK, HD), 0)
            col = j * HD + lax.broadcasted_iota(jnp.int32, (BLOCK, HD), 1)
            return jnp.where((col <= row) & (col < live), part, LOW)

        q = qc[0, r:n, columns(h)]
        at = pl.ds(ROWS_P + r, BLOCK)
        m_out[h, at, :], l_out[h, at, :], acc_out[h, at, :] = update(q, kv[0, 0, :n, :], vx[:n, :], *fresh(), mask)

    @pl.when(live > BLOCK)
    def _():
        over_heads(4, lambda h: [block(h, r) for r in (0, BLOCK)])

    @pl.when(live <= BLOCK)
    def _():
        over_heads(4, lambda h: block(h, 0))


def slab_kernel(n_slabs, step, last, *refs):
    meta, qp, qc = refs[:3]
    slabs = refs[3 : 3 + n_slabs]
    m_in, l_in, acc_in = refs[3 + n_slabs : 6 + n_slabs]
    rest = refs[6 + n_slabs :]
    vxs, outs = rest[-n_slabs:], rest[:-n_slabs]
    for vx, kv in zip(vxs, slabs):
        extend(vx, kv[1])

    live, ctx, z = meta[0], meta[1], meta[2]
    everything = tuple(range(n_slabs))

    def own_mask(j, part):
        if j == 0:
            row = lax.broadcasted_iota(jnp.int32, (BLOCK, HD), 0)
            col = lax.broadcasted_iota(jnp.int32, (BLOCK, HD), 1)
            return jnp.where(col <= row, part, LOW)
        return jnp.where((ctx ^ j) < ctx, part, LOW)

    def run(h, start, which, src=(m_in, l_in, acc_in)):
        at = pl.ds(start, BLOCK)
        first = step == 0 and start == 0
        state = fresh() if first else tuple(ref[h, at, :] for ref in src)
        if start == 0:
            q = qp[:, columns(h)]
        else:
            q = qc[0, start - ROWS_P : start - ROWS_P + BLOCK, columns(h)]
        for i in which:
            state = update(q, slabs[i][0], vxs[i][...], *state, own_mask if first else None)
        if not last:
            for ref, value in zip(outs, state):
                ref[h, at, :] = value
            return
        mixed = state[2] / state[1]
        if start == 0:
            outs[0][:, :16, columns(h)] = mixed.reshape(8, 16, HD).astype(jnp.bfloat16)
        else:
            r = start - ROWS_P
            row = r + lax.broadcasted_iota(jnp.int32, (BLOCK, HD), 0)
            mixed = jnp.where(row < live, mixed, 0.0).astype(jnp.bfloat16)
            outs[0][r // 32 : (r + BLOCK) // 32, 16:, columns(h)] = mixed.reshape(BLOCK // 32, 32, HD)

    if step == 0:
        sees = [z >= 0]
    else:
        way = 2 * (ctx & 1) - 1
        sees = [((z + (1 - 2 * i) * way * step) & 7) < z for i in range(n_slabs)]
        if step == OTHER:
            sees = [((z - way) & 7) < z]
    two = live > BLOCK
    full = functools.reduce(jnp.logical_and, sees, two)

    @pl.when(full)
    def _():
        over_heads(GQA, lambda h: [run(h, start, everything) for start in (0, BLOCK, 2 * BLOCK)])

    @pl.when(jnp.logical_not(full))
    def _():
        @pl.when(two)
        def _():
            over_heads(4, lambda h: [run(h, start, everything) for start in (BLOCK, 2 * BLOCK)])

        @pl.when(jnp.logical_not(two))
        def _():
            over_heads(4, lambda h: run(h, BLOCK, everything))
            if last:
                outs[0][4:, 16:, :] = jnp.zeros((4, 32, GQA * HD), jnp.bfloat16)

        if n_slabs == 1:

            @pl.when(sees[0])
            def _():
                over_heads(4, lambda h: run(h, 0, everything))

            if last:

                @pl.when(jnp.logical_not(sees[0]))
                def _():
                    over_heads(4, lambda h: run(h, 0, ()))
        else:
            for i in everything:
                @pl.when(sees[i])
                def _(i=i):
                    over_heads(4, lambda h: run(h, 0, (i,), outs))


OTHER = -1
VMEM = pl.BlockSpec(memory_space=pltpu.VMEM)
SMEM = pl.BlockSpec(memory_space=pltpu.SMEM)
STATE = (jax.ShapeDtypeStruct((GQA, ROWS, HD), jnp.float32),) * 3
PARAMS = pltpu.CompilerParams(vmem_limit_bytes=32 << 20)


def cost(scores):
    return pl.CostEstimate(flops=scores * 512 * 2, bytes_accessed=1 << 20, transcendentals=scores)


def attend_own(meta, qc, kv):
    return pl.pallas_call(
        own_kernel,
        in_specs=[SMEM, VMEM, VMEM],
        out_specs=(VMEM,) * 3,
        out_shape=STATE,
        scratch_shapes=[pltpu.VMEM((ROWS_C, 2 * HD), jnp.bfloat16)],
        compiler_params=PARAMS,
        cost_estimate=cost(GQA * ROWS_C * ROWS_C),
        name="own",
    )(meta, qc, kv)


def attend(meta, qp, qc, slabs, state, step, last=False):
    n = len(slabs)
    if last:
        out_specs, alias = VMEM, {}
        out_shape = jax.ShapeDtypeStruct((8, 48, GQA * HD), jnp.bfloat16)
    else:
        out_specs, out_shape = (VMEM,) * 3, STATE
        alias = {3 + n + i: i for i in range(3)}
    return pl.pallas_call(
        functools.partial(slab_kernel, n, step, last),
        in_specs=[SMEM] + [VMEM] * (n + 5),
        out_specs=out_specs,
        out_shape=out_shape,
        input_output_aliases=alias,
        scratch_shapes=[pltpu.VMEM((SLAB, 2 * HD), jnp.bfloat16)] * n,
        compiler_params=PARAMS,
        cost_estimate=cost(GQA * ROWS * SLAB * n),
        name=f"slabs{step % 9}_{n}",
    )(meta, qp, qc, *slabs, *state)


def tie(*trees):
    return lax.optimization_barrier(trees)


def body(prompt_q, prompt_kv, cont_q, cont_kv, cont_len):
    z = lax.axis_index("group")
    ctx = lax.axis_index("ctx")
    core = ctx % 2
    n_z = 8
    ring = [(g * 4 + c, ((g + (1 if c % 2 == 0 else -1)) % n_z) * 4 + c) for g in range(n_z) for c in range(4)]

    def pass_on(x):
        return lax.ppermute(x, ("group", "ctx"), ring)

    def swap(x):
        return lax.ppermute(x, "ctx", C_CORE)

    meta = jnp.stack([cont_len[0], ctx, z])
    pieces = [lax.ppermute(prompt_kv, "ctx", pairs) for pairs in (C_CORE, C_X, C_DIAG)]
    state = attend_own(meta, cont_q, cont_kv)
    pieces, state = tie(pieces, state)
    own = jnp.concatenate([prompt_kv] + pieces, axis=1)

    near = pass_on(own)
    state = attend(meta, prompt_q, cont_q, [own], state, 0)
    near, state = tie(near, state)

    other = swap(near)
    coming = pass_on(near)
    state = attend(meta, prompt_q, cont_q, [near], state, 1)
    other, state = tie(other, state)
    state = attend(meta, prompt_q, cont_q, [other], state, -1)
    near, state = tie(coming, state)

    for step in (2, 3):
        other = swap(near)
        coming = pass_on(near)
        state = attend(meta, prompt_q, cont_q, [near, other], state, step)
        near, state = tie(coming, state)
    mixed = attend(meta, prompt_q, cont_q, [near], state, 4, last=True)
    moved = lax.all_to_all(mixed, "head", split_axis=0, concat_axis=0, tiled=True)
    prompt_out = moved[:, :16].transpose(1, 0, 2).reshape(16, 8 * GQA * HD)
    cont_out = moved[:, 16:].transpose(1, 0, 2).reshape(1, 32, 8 * GQA * HD)
    return prompt_out, cont_out


def solution(mesh):
    placed = (
        P(("group", "ctx"), "head"),
        P(None, ("group", "ctx"), "head"),
        P(("group", "ctx"), None, "head"),
        P(None, ("group", "ctx"), None, "head"),
        P(("group", "ctx")),
    )
    return jax.shard_map(
        body,
        mesh=mesh,
        in_specs=placed,
        out_specs=(P(("group", "ctx", "head"), None), P(("group", "ctx"), "head", None)),
        check_vma=False,
    )
```

```python
import functools

import jax
import jax.numpy as jnp
from jax import lax
from jax.experimental import pallas as pl
from jax.experimental.pallas import tpu as pltpu
from jax.sharding import PartitionSpec as P

HD = 128
GQA = 8
ROWS_P = 128
ROWS_C = 256
ROWS = ROWS_P + ROWS_C
SLAB = 512
BLOCK = 128
LOW = -1e30
SCALE = HD**-0.5 * 1.4426950408889634
ROOM = 64 / SCALE

C_CORE = [(0, 1), (1, 0), (2, 3), (3, 2)]
C_X = [(0, 2), (2, 0), (1, 3), (3, 1)]
C_DIAG = [(0, 3), (3, 0), (1, 2), (2, 1)]


def weigh(q, keys, values, m, l, acc, mask=None):
    s = lax.dot_general(q, keys, (((1,), (1,)), ((), ())), preferred_element_type=jnp.float32)
    parts = [s[:, j : j + HD] for j in range(0, s.shape[1], HD)]
    if mask is not None:
        parts = [mask(j, part) for j, part in enumerate(parts)]
    m_new = jnp.maximum(m, jnp.max(functools.reduce(jnp.maximum, parts), axis=1, keepdims=True))
    alpha = jnp.exp2((m - m_new) * SCALE)
    l, acc = add(parts, values, m_new, l * alpha, acc * alpha)
    return m_new, l, acc


def weigh_kept(q, keys, values, m, l, acc, over):
    s = lax.dot_general(q, keys, (((1,), (1,)), ((), ())), preferred_element_type=jnp.float32)
    parts = [s[:, j : j + HD] for j in range(0, s.shape[1], HD)]
    over = jnp.maximum(over, functools.reduce(jnp.maximum, parts) - m)
    return m, *add(parts, values, m, l, acc), over


def add(parts, values, m, l, acc):
    shift = m * SCALE
    p = jnp.concatenate([jnp.exp2(part * SCALE - shift).astype(jnp.bfloat16) for part in parts], axis=1)
    pv = jnp.dot(p, values, preferred_element_type=jnp.float32)
    return l + pv[:, HD:], acc + pv[:, :HD]


def fresh():
    zero = jnp.zeros((BLOCK, HD), jnp.float32)
    return zero + LOW, zero, zero


def extend(vx, values):
    vx[:, :HD] = values
    vx[:, HD:] = jnp.ones((vx.shape[0], HD), jnp.bfloat16)


def over_heads(together, fn, over):
    def some(i, over):
        for h in range(together):
            over = fn(i * together + h, over)
        return over

    return lax.fori_loop(0, GQA // together, some, over)


def columns(h):
    return pl.ds(h * HD if isinstance(h, int) else pl.multiple_of(h * HD, HD), HD)


def spread_kernel(live, out):
    out[...] = jnp.broadcast_to(live[...], out.shape)


def spread(live):
    return pl.pallas_call(
        spread_kernel,
        out_shape=jax.ShapeDtypeStruct((8, HD), jnp.int32),
        cost_estimate=pl.CostEstimate(flops=8 << 30, bytes_accessed=16 << 20, transcendentals=0),
        name="spread",
    )(live.reshape(1, 1))


def own_kernel(meta, qc, kv, m_out, l_out, acc_out, vx):
    extend(vx, kv[1, 0])
    live = jnp.max(meta[...])

    def block(h, r):
        n = r + BLOCK

        def mask(j, part):
            row = r + lax.broadcasted_iota(jnp.int32, (BLOCK, HD), 0)
            col = j * HD + lax.broadcasted_iota(jnp.int32, (BLOCK, HD), 1)
            return jnp.where((col <= row) & (col < live), part, LOW)

        q = qc[0, r:n, columns(h)]
        at = pl.ds(ROWS_P + r, BLOCK)
        m_out[h, at, :], l_out[h, at, :], acc_out[h, at, :] = weigh(q, kv[0, 0, :n, :], vx[:n, :], *fresh(), mask)

    @pl.when(live > BLOCK)
    def _():
        for h in range(GQA):
            block(h, 0)
            block(h, BLOCK)

    @pl.when(live <= BLOCK)
    def _():
        for h in range(GQA):
            block(h, 0)


def slab_kernel(n_slabs, step, last, *refs):
    meta, qp, qc = refs[:3]
    slabs = refs[3 : 3 + n_slabs]
    m_in, l_in, acc_in = refs[3 + n_slabs : 6 + n_slabs]
    n_out = 1 if last else 3
    outs = refs[6 + n_slabs : 6 + n_slabs + n_out]
    vxs, flag = refs[6 + n_slabs + n_out : -1], refs[-1]
    for vx, kv in zip(vxs, slabs):
        extend(vx, kv[1])

    live = jnp.max(meta[...])
    ctx, z = lax.axis_index("ctx"), lax.axis_index("group")
    everything = tuple(range(n_slabs))

    def own_mask(j, part):
        if j == 0:
            row = lax.broadcasted_iota(jnp.int32, (BLOCK, HD), 0)
            col = lax.broadcasted_iota(jnp.int32, (BLOCK, HD), 1)
            return jnp.where(col <= row, part, LOW)
        return jnp.where((ctx ^ j) < ctx, part, LOW)

    def run(h, start, which, running, over):
        at = pl.ds(start, BLOCK)
        first = step == 0 and start == 0
        state = fresh() if first else tuple(ref[h, at, :] for ref in (m_in, l_in, acc_in))
        if start == 0:
            q = qp[:, columns(h)]
        else:
            q = qc[0, start - ROWS_P : start - ROWS_P + BLOCK, columns(h)]
        for i in which:
            if running or first:
                state = weigh(q, slabs[i][0], vxs[i][...], *state, own_mask if first else None)
            else:
                *state, over = weigh_kept(q, slabs[i][0], vxs[i][...], *state, over)
        if not last:
            if running or first:
                outs[0][h, at, :] = state[0]
            outs[1][h, at, :], outs[2][h, at, :] = state[1:]
            return over
        mixed = state[2] / state[1]
        if start == 0:
            outs[0][:, :16, columns(h)] = mixed.reshape(8, 16, HD).astype(jnp.bfloat16)
        else:
            r = start - ROWS_P
            row = r + lax.broadcasted_iota(jnp.int32, (BLOCK, HD), 0)
            mixed = jnp.where(row < live, mixed, 0.0).astype(jnp.bfloat16)
            outs[0][r // 32 : (r + BLOCK) // 32, 16:, columns(h)] = mixed.reshape(BLOCK // 32, 32, HD)
        return over

    way = 2 * (ctx & 1) - 1
    sees = [z >= 0] if step == 0 else [((z + (1 - 2 * i) * way * step) & 7) < z for i in range(n_slabs)]
    two = live > BLOCK
    full = functools.reduce(jnp.logical_and, sees, two)

    def everyone(running):
        together = 1 if running else 4

        def part(cond, blocks):
            @pl.when(cond)
            def _():
                def fn(h, over):
                    for start, which in blocks:
                        over = run(h, start, which, running, over)
                    return over

                flag[...] = jnp.maximum(flag[...], over_heads(together, fn, jnp.zeros((BLOCK, HD), jnp.float32)))

        flag[...] = jnp.zeros((BLOCK, HD), jnp.float32)
        part(full, [(start, everything) for start in (0, BLOCK, 2 * BLOCK)])
        rest = jnp.logical_not(full)
        part(rest & two, [(start, everything) for start in (BLOCK, 2 * BLOCK)])
        part(rest & jnp.logical_not(two), [(BLOCK, everything)])
        for code in range(2**n_slabs):
            which = tuple(i for i in everything if (code >> i) & 1)
            if step == 0 and not which:
                continue
            seen = functools.reduce(
                jnp.logical_and, [sees[i] if i in which else jnp.logical_not(sees[i]) for i in everything], rest
            )
            part(seen, [(0, which)])

    if last:

        @pl.when(jnp.logical_not(two))
        def _():
            outs[0][4:, 16:, :] = jnp.zeros((4, 32, GQA * HD), jnp.bfloat16)

    everyone(False)

    @pl.when(jnp.max(flag[...]) > ROOM)
    def _():
        everyone(True)


VMEM = pl.BlockSpec(memory_space=pltpu.VMEM)
ANY = pl.BlockSpec(memory_space=pl.ANY)
STATE = (jax.ShapeDtypeStruct((GQA, ROWS, HD), jnp.float32),) * 3
PARAMS = pltpu.CompilerParams(vmem_limit_bytes=32 << 20)


def cost(scores):
    return pl.CostEstimate(flops=scores * 512 * 2, bytes_accessed=1 << 20, transcendentals=scores)


def attend_own(meta, qc, kv):
    return pl.pallas_call(
        own_kernel,
        in_specs=[VMEM] * 3,
        out_specs=(VMEM,) * 3,
        out_shape=STATE,
        scratch_shapes=[pltpu.VMEM((ROWS_C, 2 * HD), jnp.bfloat16)],
        compiler_params=PARAMS,
        cost_estimate=cost(GQA * ROWS_C * ROWS_C),
        name="own",
    )(meta, qc, kv)


def attend(meta, qp, qc, slabs, state, step, last=False):
    n = len(slabs)
    if last:
        out_specs, alias = VMEM, {}
        out_shape = jax.ShapeDtypeStruct((8, 48, GQA * HD), jnp.bfloat16)
    else:
        out_specs, out_shape, alias = (VMEM,) * 3, STATE, {3 + n: 0}
    return pl.pallas_call(
        functools.partial(slab_kernel, n, step, last),
        in_specs=[VMEM] * (n + 6),
        out_specs=out_specs,
        out_shape=out_shape,
        input_output_aliases=alias,
        scratch_shapes=[pltpu.VMEM((SLAB, 2 * HD), jnp.bfloat16)] * n + [pltpu.VMEM((BLOCK, HD), jnp.float32)],
        compiler_params=PARAMS,
        cost_estimate=cost(GQA * ROWS * SLAB * n),
        name=f"slabs{step}",
    )(meta, qp, qc, *slabs, *state)


def lay_out_kernel(moved, prompt_out, cont_out, sems):
    copies = []
    for h in range(8):
        to = pl.ds(h * GQA * HD, GQA * HD)
        copies.append(pltpu.make_async_copy(moved.at[h, pl.ds(0, 16), :], prompt_out.at[:, to], sems.at[0, h]))
        copies.append(pltpu.make_async_copy(moved.at[h, pl.ds(16, 32), :], cont_out.at[0, :, to], sems.at[1, h]))
    for copy in copies:
        copy.start()
    for copy in copies:
        copy.wait()


def lay_out(moved):
    return pl.pallas_call(
        lay_out_kernel,
        in_specs=[ANY],
        out_specs=(ANY, ANY),
        out_shape=(
            jax.ShapeDtypeStruct((16, 8 * GQA * HD), jnp.bfloat16),
            jax.ShapeDtypeStruct((1, 32, 8 * GQA * HD), jnp.bfloat16),
        ),
        scratch_shapes=[pltpu.SemaphoreType.DMA((2, 8))],
        compiler_params=PARAMS,
        name="lay_out",
    )(moved)


def tie(*trees):
    return lax.optimization_barrier(trees)


def body(prompt_q, prompt_kv, cont_q, cont_kv, cont_len):
    n_z = 8
    ring = [(g * 4 + c, ((g + (1 if c % 2 == 0 else -1)) % n_z) * 4 + c) for g in range(n_z) for c in range(4)]

    def pass_on(x):
        return lax.ppermute(x, ("group", "ctx"), ring)

    def swap(x):
        return lax.ppermute(x, "ctx", C_CORE)

    meta = spread(cont_len)
    pieces = [lax.ppermute(prompt_kv, "ctx", pairs) for pairs in (C_CORE, C_X, C_DIAG)]
    state = attend_own(meta, cont_q, cont_kv)
    pieces, state = tie(pieces, state)
    own = jnp.concatenate([prompt_kv] + pieces, axis=1)

    near = pass_on(own)
    state = attend(meta, prompt_q, cont_q, [own], state, 0)
    near, state = tie(near, state)

    for step in (1, 2, 3):
        other = swap(near)
        coming = pass_on(near)
        state = attend(meta, prompt_q, cont_q, [near, other], state, step)
        near, state = tie(coming, state)
    mixed = attend(meta, prompt_q, cont_q, [near], state, 4, last=True)
    moved = lax.all_to_all(mixed, "head", split_axis=0, concat_axis=0, tiled=True)
    return lay_out(moved)


def solution(mesh):
    placed = (
        P(("group", "ctx"), "head"),
        P(None, ("group", "ctx"), "head"),
        P(("group", "ctx"), None, "head"),
        P(None, ("group", "ctx"), None, "head"),
        P(("group", "ctx")),
    )
    return jax.shard_map(
        body,
        mesh=mesh,
        in_specs=placed,
        out_specs=(P(("group", "ctx", "head"), None), P(("group", "ctx"), "head", None)),
        check_vma=False,
    )
```

```python
import functools

import jax
import jax.numpy as jnp
from jax import lax
from jax.experimental import pallas as pl
from jax.experimental.pallas import tpu as pltpu
from jax.sharding import PartitionSpec as P

HD = 128
GQA = 8
ROWS_P = 128
ROWS_C = 256
ROWS = ROWS_P + ROWS_C
SLAB = 512
BLOCK = 128
LOW = -1e30
SCALE = HD**-0.5 * 1.4426950408889634
ROOM = 64 / SCALE

C_CORE = [(0, 1), (1, 0), (2, 3), (3, 2)]
C_X = [(0, 2), (2, 0), (1, 3), (3, 1)]
C_DIAG = [(0, 3), (3, 0), (1, 2), (2, 1)]


def weigh(q, keys, values, m, l, acc, mask=None):
    s = lax.dot_general(q, keys, (((1,), (1,)), ((), ())), preferred_element_type=jnp.float32)
    parts = [s[:, j : j + HD] for j in range(0, s.shape[1], HD)]
    if mask is not None:
        parts = [mask(j, part) for j, part in enumerate(parts)]
    m_new = jnp.maximum(m, jnp.max(functools.reduce(jnp.maximum, parts), axis=1, keepdims=True))
    alpha = jnp.exp2((m - m_new) * SCALE)
    l, acc = add(parts, values, m_new, l * alpha, acc * alpha)
    return m_new, l, acc


def weigh_kept(q, keys, values, m, l, acc, over, mask=None):
    s = lax.dot_general(q, keys, (((1,), (1,)), ((), ())), preferred_element_type=jnp.float32)
    parts = [s[:, j : j + HD] for j in range(0, s.shape[1], HD)]
    if mask is not None:
        parts = [mask(j, part) for j, part in enumerate(parts)]
    over = jnp.maximum(over, functools.reduce(jnp.maximum, parts) - m)
    return m, *add(parts, values, m, l, acc), over


def add(parts, values, m, l, acc):
    shift = m * SCALE
    p = jnp.concatenate([jnp.exp2(part * SCALE - shift).astype(jnp.bfloat16) for part in parts], axis=1)
    pv = jnp.dot(p, values, preferred_element_type=jnp.float32)
    return l + pv[:, HD:], acc + pv[:, :HD]


def fresh():
    zero = jnp.zeros((BLOCK, HD), jnp.float32)
    return zero + LOW, zero, zero


def extend(vx, values):
    vx[:, :HD] = values
    vx[:, HD:] = jnp.ones((vx.shape[0], HD), jnp.bfloat16)


def over_heads(together, fn, over):
    def some(i, over):
        for h in range(together):
            over = fn(i * together + h, over)
        return over

    return lax.fori_loop(0, GQA // together, some, over)


def columns(h):
    return pl.ds(h * HD if isinstance(h, int) else pl.multiple_of(h * HD, HD), HD)


def spread_kernel(live, out):
    out[...] = jnp.broadcast_to(live[...], out.shape)


def spread(live):
    return pl.pallas_call(
        spread_kernel,
        out_shape=jax.ShapeDtypeStruct((8, HD), jnp.int32),
        cost_estimate=pl.CostEstimate(flops=8 << 30, bytes_accessed=16 << 20, transcendentals=0),
        name="spread",
    )(live.reshape(1, 1))


def own_kernel(meta, qc, kv, m_out, l_out, acc_out, vx):
    extend(vx, kv[1, 0])
    for h in range(GQA):
        for r in (0, BLOCK):
            n = r + BLOCK

            def mask(j, part, r=r):
                row = r + lax.broadcasted_iota(jnp.int32, (BLOCK, HD), 0)
                col = j * HD + lax.broadcasted_iota(jnp.int32, (BLOCK, HD), 1)
                return jnp.where((col <= row) & (col < meta[0:1, :]), part, LOW)

            q = qc[0, r:n, columns(h)]
            at = pl.ds(ROWS_P + r, BLOCK)
            m_out[h, at, :], l_out[h, at, :], acc_out[h, at, :] = weigh(q, kv[0, 0, :n, :], vx[:n, :], *fresh(), mask)


def slab_kernel(n_slabs, step, last, *refs):
    meta, qp, qc = refs[:3]
    slabs = refs[3 : 3 + n_slabs]
    m_in, l_in, acc_in = refs[3 + n_slabs : 6 + n_slabs]
    n_out = 1 if last else 3
    outs = refs[6 + n_slabs : 6 + n_slabs + n_out]
    vxs, flag = refs[6 + n_slabs + n_out : -1], refs[-1]
    for vx, kv in zip(vxs, slabs):
        extend(vx, kv[1])

    ctx, z = lax.axis_index("ctx"), lax.axis_index("group")

    def own_mask(j, part):
        if j == 0:
            row = lax.broadcasted_iota(jnp.int32, (BLOCK, HD), 0)
            col = lax.broadcasted_iota(jnp.int32, (BLOCK, HD), 1)
            return jnp.where(col <= row, part, LOW)
        return jnp.where((ctx ^ j) < ctx, part, LOW)

    def run(h, r, running, over, partly=False):
        at = pl.ds(0 if r is None else ROWS_P + r, BLOCK)
        first = step == 0 and r is None
        state = fresh() if first else tuple(ref[h, at, :] for ref in (m_in, l_in, acc_in))
        q = qp[:, columns(h)] if r is None else qc[0, pl.ds(r, BLOCK), columns(h)]
        for i in range(n_slabs) if partly is not None else ():
            mask = own_mask if first else None
            if partly:
                mask = lambda j, part, i=i: jnp.where(sees[i], part, LOW)
            if running or first:
                state = weigh(q, slabs[i][0], vxs[i][...], *state, mask)
            else:
                *state, over = weigh_kept(q, slabs[i][0], vxs[i][...], *state, over, mask)
        if not last:
            if running or first:
                outs[0][h, at, :] = state[0]
            outs[1][h, at, :], outs[2][h, at, :] = state[1:]
            return over
        mixed = state[2] / state[1]
        if r is None:
            outs[0][:, :16, columns(h)] = mixed.reshape(8, 16, HD).astype(jnp.bfloat16)
        else:
            row = r + lax.broadcasted_iota(jnp.int32, (BLOCK, HD), 0)
            mixed = jnp.where(row < meta[0:1, :], mixed, 0.0).astype(jnp.bfloat16)
            outs[0][pl.ds(r // 32, BLOCK // 32), 16:, columns(h)] = mixed.reshape(BLOCK // 32, 32, HD)
        return over

    way = 2 * (ctx & 1) - 1
    sees = [jnp.bool_(True)] if step == 0 else [((z + (1 - 2 * i) * way * step) & 7) < z for i in range(n_slabs)]
    none = jnp.zeros((BLOCK, HD), jnp.float32)

    def rows(blocks, running=False, partly=False):
        def head(h, over):
            for r in blocks:
                over = run(h, r, running, over, partly)
            return over

        return over_heads(1 if running else 4, head, none)

    if step == 0:
        flag[...] = rows((None, 0, BLOCK))
    else:
        full = functools.reduce(jnp.logical_and, sees)
        some = functools.reduce(jnp.logical_or, sees)

        @pl.when(full)
        def _():
            flag[...] = rows((None, 0, BLOCK))

        @pl.when(jnp.logical_not(full))
        def _():
            flag[...] = rows((0, BLOCK))
            if n_slabs > 1:

                @pl.when(some)
                def _():
                    flag[...] = jnp.maximum(flag[...], rows((None,), partly=True))

            @pl.when(jnp.logical_not(some))
            def _():
                if last:
                    rows((None,), partly=None)
                else:
                    for before, after in ((l_in, outs[1]), (acc_in, outs[2])):
                        after[:, :ROWS_P, :] = before[:, :ROWS_P, :]

    @pl.when(jnp.max(flag[...]) > ROOM)
    def _():
        rows((0, BLOCK), running=True)
        rows((None,), running=True, partly=step != 0)


VMEM = pl.BlockSpec(memory_space=pltpu.VMEM)
ANY = pl.BlockSpec(memory_space=pl.ANY)
STATE = (jax.ShapeDtypeStruct((GQA, ROWS, HD), jnp.float32),) * 3
PARAMS = pltpu.CompilerParams(vmem_limit_bytes=32 << 20)


def cost(scores):
    return pl.CostEstimate(flops=scores * 512 * 2, bytes_accessed=1 << 20, transcendentals=scores)


def attend_own(meta, qc, kv):
    return pl.pallas_call(
        own_kernel,
        in_specs=[VMEM] * 3,
        out_specs=(VMEM,) * 3,
        out_shape=STATE,
        scratch_shapes=[pltpu.VMEM((ROWS_C, 2 * HD), jnp.bfloat16)],
        compiler_params=PARAMS,
        cost_estimate=cost(GQA * ROWS_C * ROWS_C),
        name="own",
    )(meta, qc, kv)


def attend(meta, qp, qc, slabs, state, step, last=False):
    n = len(slabs)
    if last:
        out_specs, alias = VMEM, {}
        out_shape = jax.ShapeDtypeStruct((8, 48, GQA * HD), jnp.bfloat16)
    else:
        out_specs, out_shape, alias = (VMEM,) * 3, STATE, {3 + n: 0}
    return pl.pallas_call(
        functools.partial(slab_kernel, n, step, last),
        in_specs=[VMEM] * (n + 6),
        out_specs=out_specs,
        out_shape=out_shape,
        input_output_aliases=alias,
        scratch_shapes=[pltpu.VMEM((SLAB, 2 * HD), jnp.bfloat16)] * n + [pltpu.VMEM((BLOCK, HD), jnp.float32)],
        compiler_params=PARAMS,
        cost_estimate=cost(GQA * ROWS * SLAB * n),
        name=f"slabs{step}",
    )(meta, qp, qc, *slabs, *state)


def lay_out_kernel(moved, prompt_out, cont_out, sems):
    copies = []
    for h in range(8):
        to = pl.ds(h * GQA * HD, GQA * HD)
        copies.append(pltpu.make_async_copy(moved.at[h, pl.ds(0, 16), :], prompt_out.at[:, to], sems.at[0, h]))
        copies.append(pltpu.make_async_copy(moved.at[h, pl.ds(16, 32), :], cont_out.at[0, :, to], sems.at[1, h]))
    for copy in copies:
        copy.start()
    for copy in copies:
        copy.wait()


def lay_out(moved):
    return pl.pallas_call(
        lay_out_kernel,
        in_specs=[ANY],
        out_specs=(ANY, ANY),
        out_shape=(
            jax.ShapeDtypeStruct((16, 8 * GQA * HD), jnp.bfloat16),
            jax.ShapeDtypeStruct((1, 32, 8 * GQA * HD), jnp.bfloat16),
        ),
        scratch_shapes=[pltpu.SemaphoreType.DMA((2, 8))],
        compiler_params=PARAMS,
        name="lay_out",
    )(moved)


def tie(*trees):
    return lax.optimization_barrier(trees)


def body(prompt_q, prompt_kv, cont_q, cont_kv, cont_len):
    n_z = 8
    ring = [(g * 4 + c, ((g + (1 if c % 2 == 0 else -1)) % n_z) * 4 + c) for g in range(n_z) for c in range(4)]

    def pass_on(x):
        return lax.ppermute(x, ("group", "ctx"), ring)

    def swap(x):
        return lax.ppermute(x, "ctx", C_CORE)

    meta = spread(cont_len)
    pieces = [lax.ppermute(prompt_kv, "ctx", pairs) for pairs in (C_CORE, C_X, C_DIAG)]
    state = attend_own(meta, cont_q, cont_kv)
    pieces, state = tie(pieces, state)
    own = jnp.concatenate([prompt_kv] + pieces, axis=1)

    near = pass_on(own)
    state = attend(meta, prompt_q, cont_q, [own], state, 0)
    near, state = tie(near, state)

    for step in (1, 2, 3):
        other = swap(near)
        coming = pass_on(near)
        state = attend(meta, prompt_q, cont_q, [near, other], state, step)
        near, state = tie(coming, state)
    mixed = attend(meta, prompt_q, cont_q, [near], state, 4, last=True)
    moved = lax.all_to_all(mixed, "head", split_axis=0, concat_axis=0, tiled=True)
    return lay_out(moved)


def solution(mesh):
    placed = (
        P(("group", "ctx"), "head"),
        P(None, ("group", "ctx"), "head"),
        P(("group", "ctx"), None, "head"),
        P(None, ("group", "ctx"), None, "head"),
        P(("group", "ctx")),
    )
    return jax.shard_map(
        body,
        mesh=mesh,
        in_specs=placed,
        out_specs=(P(("group", "ctx", "head"), None), P(("group", "ctx"), "head", None)),
        check_vma=False,
    )
```

```python
import functools

import jax
import jax.numpy as jnp
from jax import lax
from jax.experimental import pallas as pl
from jax.experimental.pallas import tpu as pltpu
from jax.sharding import PartitionSpec as P

HD = 128
GQA = 8
ROWS_P = 128
ROWS_C = 256
ROWS = ROWS_P + ROWS_C
SLAB = 512
BLOCK = 128
LOW = -1e30
SCALE = HD**-0.5 * 1.4426950408889634
ROOM = 64 / SCALE

C_CORE = [(0, 1), (1, 0), (2, 3), (3, 2)]
C_X = [(0, 2), (2, 0), (1, 3), (3, 1)]
C_DIAG = [(0, 3), (3, 0), (1, 2), (2, 1)]


def weigh(q, keys, values, m, l, acc, mask=None):
    s = lax.dot_general(q, keys, (((1,), (1,)), ((), ())), preferred_element_type=jnp.float32)
    parts = [s[:, j : j + HD] for j in range(0, s.shape[1], HD)]
    if mask is not None:
        parts = [mask(j, part) for j, part in enumerate(parts)]
    m_new = jnp.maximum(m, jnp.max(functools.reduce(jnp.maximum, parts), axis=1, keepdims=True))
    alpha = jnp.exp2((m - m_new) * SCALE)
    l, acc = add(parts, values, m_new, l * alpha, acc * alpha)
    return m_new, l, acc


def weigh_kept(q, keys, values, m, l, acc, over, mask=None):
    s = lax.dot_general(q, keys, (((1,), (1,)), ((), ())), preferred_element_type=jnp.float32)
    parts = [s[:, j : j + HD] for j in range(0, s.shape[1], HD)]
    if mask is not None:
        parts = [mask(j, part) for j, part in enumerate(parts)]
    over = jnp.maximum(over, functools.reduce(jnp.maximum, parts) - m)
    return m, *add(parts, values, m, l, acc), over


def add(parts, values, m, l, acc):
    shift = m * SCALE
    p = jnp.concatenate([jnp.exp2(part * SCALE - shift).astype(jnp.bfloat16) for part in parts], axis=1)
    pv = jnp.dot(p, values, preferred_element_type=jnp.float32)
    return l + pv[:, HD:], acc + pv[:, :HD]


def fresh():
    zero = jnp.zeros((BLOCK, HD), jnp.float32)
    return zero + LOW, zero, zero


def extend(vx, values):
    vx[:, :HD] = values
    vx[:, HD:] = jnp.ones((vx.shape[0], HD), jnp.bfloat16)


def over_heads(together, fn, over):
    def some(i, over):
        for h in range(together):
            over = fn(i * together + h, over)
        return over

    return lax.fori_loop(0, GQA // together, some, over)


def columns(h):
    return pl.ds(h * HD if isinstance(h, int) else pl.multiple_of(h * HD, HD), HD)


def spread_kernel(live, out):
    out[...] = jnp.broadcast_to(live[...], out.shape)


def spread(live):
    return pl.pallas_call(
        spread_kernel,
        out_shape=jax.ShapeDtypeStruct((8, HD), jnp.int32),
        cost_estimate=pl.CostEstimate(flops=8 << 30, bytes_accessed=16 << 20, transcendentals=0),
        name="spread",
    )(live.reshape(1, 1))


def own_kernel(meta, qc, kv, m_out, l_out, acc_out, vx):
    extend(vx, kv[1, 0])
    for h in range(GQA):
        for r in (0, BLOCK):
            n = r + BLOCK

            def mask(j, part, r=r):
                row = r + lax.broadcasted_iota(jnp.int32, (BLOCK, HD), 0)
                col = j * HD + lax.broadcasted_iota(jnp.int32, (BLOCK, HD), 1)
                return jnp.where((col <= row) & (col < meta[0:1, :]), part, LOW)

            q = qc[0, r:n, columns(h)]
            at = pl.ds(ROWS_P + r, BLOCK)
            m_out[h, at, :], l_out[h, at, :], acc_out[h, at, :] = weigh(q, kv[0, 0, :n, :], vx[:n, :], *fresh(), mask)


def sees(step, i):
    z = lax.axis_index("group")
    way = 2 * (lax.axis_index("ctx") & 1) - 1
    return ((z + (1 - 2 * i) * way * step) & 7) < z


def read(refs, h, at):
    return tuple(ref[h, at, :] for ref in refs)


def write(refs, h, at, values):
    for ref, value in zip(refs, values):
        ref[h, at, :] = value


def place(r):
    return pl.ds(0 if r is None else ROWS_P + r, BLOCK)


def queries(qp, qc, h, r):
    return qp[:, columns(h)] if r is None else qc[0, pl.ds(r, BLOCK), columns(h)]


def first_kernel(qp, qc, slab, m_in, l_in, acc_in, m_out, l_out, acc_out, vx):
    extend(vx, slab[1])
    ctx = lax.axis_index("ctx")

    def mask(j, part):
        if j == 0:
            row = lax.broadcasted_iota(jnp.int32, (BLOCK, HD), 0)
            col = lax.broadcasted_iota(jnp.int32, (BLOCK, HD), 1)
            return jnp.where(col <= row, part, LOW)
        return jnp.where((ctx ^ j) < ctx, part, LOW)

    def head(h, carry):
        for r in (None, 0, BLOCK):
            state = fresh() if r is None else read((m_in, l_in, acc_in), h, place(r))
            state = weigh(queries(qp, qc, h, r), slab[0], vx[...], *state, mask if r is None else None)
            write((m_out, l_out, acc_out), h, place(r), state)
        return carry

    over_heads(4, head, 0)


def rows_kept(blocks, qp, qc, slabs, vxs, m_ref, src, put, seen=None):
    def head(h, over):
        for r in blocks:
            m, l, acc = read((m_ref, *src), h, place(r))
            for i, slab in enumerate(slabs):
                mask = None if seen is None else lambda j, part, i=i: jnp.where(seen[i], part, LOW)
                m, l, acc, over = weigh_kept(queries(qp, qc, h, r), slab[0], vxs[i][...], m, l, acc, over, mask)
            put(h, r, l, acc)
        return over

    return over_heads(4, head, jnp.zeros((BLOCK, HD), jnp.float32))


def middle_kernel(step, qp, qc, near, other, m_ref, l_in, acc_in, over_in, l_out, acc_out, over_out, *vxs):
    slabs = (near, other)
    for vx, kv in zip(vxs, slabs):
        extend(vx, kv[1])
    seen = [sees(step, i) for i in range(2)]

    def put(h, r, l, acc):
        write((l_out, acc_out), h, place(r), (l, acc))

    def rows(blocks, seen=None):
        over = rows_kept(blocks, qp, qc, slabs, vxs, m_ref, (l_in, acc_in), put, seen)
        over_out[...] = jnp.maximum(over_out[...], over)

    over_out[...] = jnp.zeros((BLOCK, HD), jnp.float32) if step == 1 else over_in[...]
    full = seen[0] & seen[1]

    @pl.when(full)
    def _():
        rows((None, 0, BLOCK))

    @pl.when(jnp.logical_not(full))
    def _():
        rows((0, BLOCK))
        some = seen[0] | seen[1]

        @pl.when(some)
        def _():
            rows((None,), seen)

        if step == 1:

            @pl.when(jnp.logical_not(some))
            def _():
                l_out[:, :ROWS_P, :] = l_in[:, :ROWS_P, :]
                acc_out[:, :ROWS_P, :] = acc_in[:, :ROWS_P, :]


def last_kernel(meta, qp, qc, *refs):
    slabs, far = refs[:7], refs[6]
    m_ref, l_in, acc_in, over_in, l_first, acc_first, out, vx, flag, *redo = refs[7:]
    extend(vx, far[1])
    seen = sees(4, 0)

    def put(h, r, l, acc):
        mixed = acc / l
        if r is None:
            out[:, :16, columns(h)] = mixed.reshape(8, 16, HD).astype(jnp.bfloat16)
        else:
            row = r + lax.broadcasted_iota(jnp.int32, (BLOCK, HD), 0)
            mixed = jnp.where(row < meta[0:1, :], mixed, 0.0).astype(jnp.bfloat16)
            out[pl.ds(r // 32, BLOCK // 32), 16:, columns(h)] = mixed.reshape(BLOCK // 32, 32, HD)

    def rows(blocks):
        over = rows_kept(blocks, qp, qc, (far,), (vx,), m_ref, (l_in, acc_in), put)
        flag[...] = jnp.maximum(over_in[...], over)

    @pl.when(seen)
    def _():
        rows((None, 0, BLOCK))

    @pl.when(jnp.logical_not(seen))
    def _():
        rows((0, BLOCK))

        def head(h, carry):
            put(h, None, l_in[h, place(None), :], acc_in[h, place(None), :])
            return carry

        over_heads(4, head, 0)

    @pl.when(jnp.max(flag[...]) > ROOM)
    def _():
        for n, slab in enumerate(slabs):
            extend(vx, slab[1])
            visible = sees(n // 2 + 1, n % 2)

            def head(h, carry, n=n, slab=slab, visible=visible):
                for r in (None, 0, BLOCK):
                    state = read((m_ref, l_first, acc_first) if n == 0 else redo, h, place(r))
                    mask = (lambda j, part: jnp.where(visible, part, LOW)) if r is None else None
                    state = weigh(queries(qp, qc, h, r), slab[0], vx[...], *state, mask)
                    write(redo, h, place(r), state)
                    if n == 6:
                        put(h, r, *state[1:])
                return carry

            over_heads(1, head, 0)


VMEM = pl.BlockSpec(memory_space=pltpu.VMEM)
ANY = pl.BlockSpec(memory_space=pl.ANY)
STATE = (jax.ShapeDtypeStruct((GQA, ROWS, HD), jnp.float32),) * 3
EXCESS = jax.ShapeDtypeStruct((BLOCK, HD), jnp.float32)
PARAMS = pltpu.CompilerParams(vmem_limit_bytes=32 << 20)


def cost(scores):
    return pl.CostEstimate(flops=scores * 512 * 2, bytes_accessed=1 << 20, transcendentals=scores)


def call(kernel, name, scores, n_in, out_shape, alias, scratch, more=()):
    return pl.pallas_call(
        kernel,
        in_specs=[VMEM] * n_in,
        out_specs=jax.tree.map(lambda _: VMEM, out_shape),
        out_shape=out_shape,
        input_output_aliases=alias,
        scratch_shapes=[pltpu.VMEM((n, 2 * HD), jnp.bfloat16) for n in scratch] + [pltpu.VMEM(x.shape, x.dtype) for x in more],
        compiler_params=PARAMS,
        cost_estimate=cost(scores),
        name=name,
    )


def attend_own(*args):
    return call(own_kernel, "own", GQA * ROWS_C * ROWS_C, 3, STATE, {}, [ROWS_C])(*args)


def attend_first(*args):
    return call(first_kernel, "first", GQA * ROWS * SLAB, 6, STATE, {3: 0, 4: 1, 5: 2}, [SLAB])(*args)


def attend_middle(step, *args):
    alias = {} if step == 1 else {5: 0, 6: 1, 7: 2}
    kernel = functools.partial(middle_kernel, step)
    return call(kernel, f"middle{step}", GQA * ROWS * SLAB * 2, 8, (*STATE[1:], EXCESS), alias, [SLAB] * 2)(*args)


def attend_last(*args):
    out = jax.ShapeDtypeStruct((8, 48, GQA * HD), jnp.bfloat16)
    return call(last_kernel, "last", GQA * ROWS * SLAB, 16, out, {}, [SLAB], (EXCESS, *STATE))(*args)


def lay_out_kernel(moved, prompt_out, cont_out, sems):
    copies = []
    for h in range(8):
        to = pl.ds(h * GQA * HD, GQA * HD)
        copies.append(pltpu.make_async_copy(moved.at[h, pl.ds(0, 16), :], prompt_out.at[:, to], sems.at[0, h]))
        copies.append(pltpu.make_async_copy(moved.at[h, pl.ds(16, 32), :], cont_out.at[0, :, to], sems.at[1, h]))
    for copy in copies:
        copy.start()
    for copy in copies:
        copy.wait()


def lay_out(moved):
    return pl.pallas_call(
        lay_out_kernel,
        in_specs=[ANY],
        out_specs=(ANY, ANY),
        out_shape=(
            jax.ShapeDtypeStruct((16, 8 * GQA * HD), jnp.bfloat16),
            jax.ShapeDtypeStruct((1, 32, 8 * GQA * HD), jnp.bfloat16),
        ),
        scratch_shapes=[pltpu.SemaphoreType.DMA((2, 8))],
        compiler_params=PARAMS,
        name="lay_out",
    )(moved)


def tie(*trees):
    return lax.optimization_barrier(trees)


def body(prompt_q, prompt_kv, cont_q, cont_kv, cont_len):
    n_z = 8
    ring = [(g * 4 + c, ((g + (1 if c % 2 == 0 else -1)) % n_z) * 4 + c) for g in range(n_z) for c in range(4)]

    def pass_on(x):
        return lax.ppermute(x, ("group", "ctx"), ring)

    def swap(x):
        return lax.ppermute(x, "ctx", C_CORE)

    meta = spread(cont_len)
    pieces = [lax.ppermute(prompt_kv, "ctx", pairs) for pairs in (C_CORE, C_X, C_DIAG)]
    state = attend_own(meta, cont_q, cont_kv)
    pieces, state = tie(pieces, state)
    own = jnp.concatenate([prompt_kv] + pieces, axis=1)

    near = pass_on(own)
    m, l, acc = attend_first(prompt_q, cont_q, own, *state)
    near, m, l, acc = tie(near, m, l, acc)
    l_first, acc_first = l, acc

    over, slabs = jnp.zeros(EXCESS.shape, EXCESS.dtype), []
    for step in (1, 2, 3):
        other = swap(near)
        slabs += [near, other]
        coming = pass_on(near)
        l, acc, over = attend_middle(step, prompt_q, cont_q, near, other, m, l, acc, over)
        near, l, acc, over = tie(coming, l, acc, over)
    mixed = attend_last(meta, prompt_q, cont_q, *slabs, near, m, l, acc, over, l_first, acc_first)
    moved = lax.all_to_all(mixed, "head", split_axis=0, concat_axis=0, tiled=True)
    return lay_out(moved)


def solution(mesh):
    placed = (
        P(("group", "ctx"), "head"),
        P(None, ("group", "ctx"), "head"),
        P(("group", "ctx"), None, "head"),
        P(None, ("group", "ctx"), None, "head"),
        P(("group", "ctx")),
    )
    return jax.shard_map(
        body,
        mesh=mesh,
        in_specs=placed,
        out_specs=(P(("group", "ctx", "head"), None), P(("group", "ctx"), "head", None)),
        check_vma=False,
    )
```

```python
import functools

import jax
import jax.numpy as jnp
from jax import lax
from jax.experimental import pallas as pl
from jax.experimental.pallas import tpu as pltpu
from jax.sharding import PartitionSpec as P

HD = 128
GQA = 8
ROWS_P = 128
ROWS_C = 256
ROWS = ROWS_P + ROWS_C
SLAB = 512
BLOCK = 128
LOW = -1e30
SCALE = HD**-0.5 * 1.4426950408889634
ROOM = 64 / SCALE

C_CORE = [(0, 1), (1, 0), (2, 3), (3, 2)]
C_X = [(0, 2), (2, 0), (1, 3), (3, 1)]
C_DIAG = [(0, 3), (3, 0), (1, 2), (2, 1)]


def weigh(q, keys, values, m, l, acc, mask=None):
    s = lax.dot_general(q, keys, (((1,), (1,)), ((), ())), preferred_element_type=jnp.float32)
    parts = [s[:, j : j + HD] for j in range(0, s.shape[1], HD)]
    if mask is not None:
        parts = [mask(j, part) for j, part in enumerate(parts)]
    m_new = jnp.maximum(m, jnp.max(functools.reduce(jnp.maximum, parts), axis=1, keepdims=True))
    alpha = jnp.exp2((m - m_new) * SCALE)
    l, acc = add(parts, values, m_new, l * alpha, acc * alpha)
    return m_new, l, acc


def weigh_kept(q, keys, values, m, l, acc, over, mask=None):
    s = lax.dot_general(q, keys, (((1,), (1,)), ((), ())), preferred_element_type=jnp.float32)
    parts = [s[:, j : j + HD] for j in range(0, s.shape[1], HD)]
    if mask is not None:
        parts = [mask(j, part) for j, part in enumerate(parts)]
    over = jnp.maximum(over, functools.reduce(jnp.maximum, parts) - m)
    return m, *add(parts, values, m, l, acc), over


def add(parts, values, m, l, acc):
    shift = m * SCALE
    p = jnp.concatenate([jnp.exp2(part * SCALE - shift).astype(jnp.bfloat16) for part in parts], axis=1)
    pv = jnp.dot(p, values, preferred_element_type=jnp.float32)
    return l + pv[:, HD:], acc + pv[:, :HD]


def fresh():
    zero = jnp.zeros((BLOCK, HD), jnp.float32)
    return zero + LOW, zero, zero


def extend(vx, values):
    vx[:, :HD] = values
    vx[:, HD:] = jnp.ones((vx.shape[0], HD), jnp.bfloat16)


def over_heads(together, fn, over):
    def some(i, over):
        for h in range(together):
            over = fn(i * together + h, over)
        return over

    return lax.fori_loop(0, GQA // together, some, over)


def columns(h):
    return pl.ds(h * HD if isinstance(h, int) else pl.multiple_of(h * HD, HD), HD)


def spread_kernel(live, out):
    out[...] = jnp.broadcast_to(live[...], out.shape)


def spread(live):
    return pl.pallas_call(
        spread_kernel,
        out_shape=jax.ShapeDtypeStruct((8, HD), jnp.int32),
        cost_estimate=pl.CostEstimate(flops=8 << 30, bytes_accessed=16 << 20, transcendentals=0),
        name="spread",
    )(live.reshape(1, 1))


def own_kernel(meta, qc, kv, m_out, l_out, acc_out, vx):
    extend(vx, kv[1, 0])
    for h in range(GQA):
        for r in (0, BLOCK):
            n = r + BLOCK

            def mask(j, part, r=r):
                row = r + lax.broadcasted_iota(jnp.int32, (BLOCK, HD), 0)
                col = j * HD + lax.broadcasted_iota(jnp.int32, (BLOCK, HD), 1)
                return jnp.where((col <= row) & (col < meta[0:1, :]), part, LOW)

            q = qc[0, r:n, columns(h)]
            at = pl.ds(ROWS_P + r, BLOCK)
            m_out[h, at, :], l_out[h, at, :], acc_out[h, at, :] = weigh(q, kv[0, 0, :n, :], vx[:n, :], *fresh(), mask)


def sees(step, i):
    z = lax.axis_index("group")
    way = 2 * (lax.axis_index("ctx") & 1) - 1
    return ((z + (1 - 2 * i) * way * step) & 7) < z


def read(refs, h, at):
    return tuple(ref[h, at, :] for ref in refs)


def write(refs, h, at, values):
    for ref, value in zip(refs, values):
        ref[h, at, :] = value


def place(r):
    return pl.ds(0 if r is None else ROWS_P + r, BLOCK)


def queries(qp, qc, h, r):
    return qp[:, columns(h)] if r is None else qc[0, pl.ds(r, BLOCK), columns(h)]


def first_kernel(qp, qc, slab, m_in, l_in, acc_in, m_out, l_out, acc_out, vx):
    extend(vx, slab[1])
    ctx = lax.axis_index("ctx")

    def mask(j, part):
        if j == 0:
            row = lax.broadcasted_iota(jnp.int32, (BLOCK, HD), 0)
            col = lax.broadcasted_iota(jnp.int32, (BLOCK, HD), 1)
            return jnp.where(col <= row, part, LOW)
        return jnp.where((ctx ^ j) < ctx, part, LOW)

    def head(h, carry):
        for r in (None, 0, BLOCK):
            state = fresh() if r is None else read((m_in, l_in, acc_in), h, place(r))
            state = weigh(queries(qp, qc, h, r), slab[0], vx[...], *state, mask if r is None else None)
            write((m_out, l_out, acc_out), h, place(r), state)
        return carry

    over_heads(4, head, 0)


def rows_kept(blocks, qp, qc, slabs, vxs, m_ref, src, put, seen=None):
    def head(h, over):
        for r in blocks:
            m, l, acc = read((m_ref, *src), h, place(r))
            for i, slab in enumerate(slabs):
                mask = None if seen is None else lambda j, part, i=i: jnp.where(seen[i], part, LOW)
                m, l, acc, over = weigh_kept(queries(qp, qc, h, r), slab[0], vxs[i][...], m, l, acc, over, mask)
            put(h, r, l, acc)
        return over

    return over_heads(4, head, jnp.zeros((BLOCK, HD), jnp.float32))


def middle_kernel(step, qp, qc, near, other, m_ref, l_in, acc_in, over_in, l_out, acc_out, over_out, *vxs):
    slabs = (near, other)
    for vx, kv in zip(vxs, slabs):
        extend(vx, kv[1])
    seen = [sees(step, i) for i in range(2)]

    def put(h, r, l, acc):
        write((l_out, acc_out), h, place(r), (l, acc))

    def rows(blocks, seen=None):
        over = rows_kept(blocks, qp, qc, slabs, vxs, m_ref, (l_in, acc_in), put, seen)
        over_out[...] = jnp.maximum(over_out[...], over)

    over_out[...] = jnp.zeros((BLOCK, HD), jnp.float32) if step == 1 else over_in[...]
    full = seen[0] & seen[1]

    @pl.when(full)
    def _():
        rows((None, 0, BLOCK))

    @pl.when(jnp.logical_not(full))
    def _():
        rows((0, BLOCK))
        some = seen[0] | seen[1]

        @pl.when(some)
        def _():
            rows((None,), seen)

        if step == 1:

            @pl.when(jnp.logical_not(some))
            def _():
                l_out[:, :ROWS_P, :] = l_in[:, :ROWS_P, :]
                acc_out[:, :ROWS_P, :] = acc_in[:, :ROWS_P, :]


def last_kernel(meta, qp, qc, *refs):
    slabs, far = refs[:7], refs[6]
    m_ref, l_in, acc_in, over_in, l_first, acc_first, out, vx, flag, *redo = refs[7:]
    extend(vx, far[1])
    seen = sees(4, 0)

    def put(h, r, l, acc):
        mixed = acc / l
        if r is None:
            out[:, :16, columns(h)] = mixed.reshape(8, 16, HD).astype(jnp.bfloat16)
        else:
            row = r + lax.broadcasted_iota(jnp.int32, (BLOCK, HD), 0)
            mixed = jnp.where(row < meta[0:1, :], mixed, 0.0).astype(jnp.bfloat16)
            out[pl.ds(r // 32, BLOCK // 32), 16:, columns(h)] = mixed.reshape(BLOCK // 32, 32, HD)

    def rows(blocks):
        over = rows_kept(blocks, qp, qc, (far,), (vx,), m_ref, (l_in, acc_in), put)
        flag[...] = jnp.maximum(over_in[...], over)

    @pl.when(seen)
    def _():
        rows((None, 0, BLOCK))

    @pl.when(jnp.logical_not(seen))
    def _():
        rows((0, BLOCK))

        def head(h, carry):
            put(h, None, l_in[h, place(None), :], acc_in[h, place(None), :])
            return carry

        over_heads(4, head, 0)

    @pl.when(jnp.max(flag[...]) > ROOM)
    def _():
        for n, slab in enumerate(slabs):
            extend(vx, slab[1])
            visible = sees(n // 2 + 1, n % 2)

            def head(h, carry, n=n, slab=slab, visible=visible):
                for r in (None, 0, BLOCK):
                    state = read((m_ref, l_first, acc_first) if n == 0 else redo, h, place(r))
                    mask = (lambda j, part: jnp.where(visible, part, LOW)) if r is None else None
                    state = weigh(queries(qp, qc, h, r), slab[0], vx[...], *state, mask)
                    write(redo, h, place(r), state)
                    if n == 6:
                        put(h, r, *state[1:])
                return carry

            over_heads(1, head, 0)


VMEM = pl.BlockSpec(memory_space=pltpu.VMEM)
ANY = pl.BlockSpec(memory_space=pl.ANY)
STATE = (jax.ShapeDtypeStruct((GQA, ROWS, HD), jnp.float32),) * 3
EXCESS = jax.ShapeDtypeStruct((BLOCK, HD), jnp.float32)
PARAMS = pltpu.CompilerParams(vmem_limit_bytes=32 << 20)


def cost(scores):
    return pl.CostEstimate(flops=scores * 512 * 2, bytes_accessed=1 << 20, transcendentals=scores)


def call(kernel, name, scores, n_in, out_shape, alias, scratch, more=()):
    return pl.pallas_call(
        kernel,
        in_specs=[VMEM] * n_in,
        out_specs=jax.tree.map(lambda _: VMEM, out_shape),
        out_shape=out_shape,
        input_output_aliases=alias,
        scratch_shapes=[pltpu.VMEM((n, 2 * HD), jnp.bfloat16) for n in scratch] + [pltpu.VMEM(x.shape, x.dtype) for x in more],
        compiler_params=PARAMS,
        cost_estimate=cost(scores),
        name=name,
    )


def attend_own(*args):
    return call(own_kernel, "own", GQA * ROWS_C * ROWS_C, 3, STATE, {}, [ROWS_C])(*args)


def attend_first(*args):
    return call(first_kernel, "first", GQA * ROWS * SLAB, 6, STATE, {3: 0, 4: 1, 5: 2}, [SLAB])(*args)


def attend_middle(step, *args):
    alias = {} if step == 1 else {5: 0, 6: 1, 7: 2}
    kernel = functools.partial(middle_kernel, step)
    return call(kernel, f"middle{step}", GQA * ROWS * SLAB * 2, 8, (*STATE[1:], EXCESS), alias, [SLAB] * 2)(*args)


def attend_last(*args):
    out = jax.ShapeDtypeStruct((8, 48, GQA * HD), jnp.bfloat16)
    return call(last_kernel, "last", GQA * ROWS * SLAB, 16, out, {}, [SLAB], (EXCESS, *STATE))(*args)


def lay_out_kernel(moved, prompt_out, cont_out, sems):
    copies = []
    for h in range(8):
        to = pl.ds(h * GQA * HD, GQA * HD)
        copies.append(pltpu.make_async_copy(moved.at[h, pl.ds(0, 16), :], prompt_out.at[:, to], sems.at[0, h]))
        copies.append(pltpu.make_async_copy(moved.at[h, pl.ds(16, 32), :], cont_out.at[0, :, to], sems.at[1, h]))
    for copy in copies:
        copy.start()
    for copy in copies:
        copy.wait()


def lay_out(moved):
    return pl.pallas_call(
        lay_out_kernel,
        in_specs=[ANY],
        out_specs=(ANY, ANY),
        out_shape=(
            jax.ShapeDtypeStruct((16, 8 * GQA * HD), jnp.bfloat16),
            jax.ShapeDtypeStruct((1, 32, 8 * GQA * HD), jnp.bfloat16),
        ),
        scratch_shapes=[pltpu.SemaphoreType.DMA((2, 8))],
        compiler_params=PARAMS,
        name="lay_out",
    )(moved)


def tie(*trees):
    return lax.optimization_barrier(trees)


def body(prompt_q, prompt_kv, cont_q, cont_kv, cont_len):
    n_z = 8
    ring = [(g * 4 + c, ((g + (1 if c % 2 == 0 else -1)) % n_z) * 4 + c) for g in range(n_z) for c in range(4)]

    def pass_on(x):
        return lax.ppermute(x, ("group", "ctx"), ring)

    def swap(x):
        return lax.ppermute(x, "ctx", C_CORE)

    meta = spread(cont_len)
    partner, across, diagonal = (lax.ppermute(prompt_kv, "ctx", pairs) for pairs in (C_CORE, C_X, C_DIAG))
    chip = jnp.concatenate([prompt_kv, partner], axis=1)
    chip, meta = tie(chip, meta)
    near_chip = pass_on(chip)
    state = attend_own(meta, cont_q, cont_kv)
    across, diagonal, state = tie(across, diagonal, state)
    other_chip = jnp.concatenate([across, diagonal], axis=1)
    near_other = pass_on(other_chip)
    own = jnp.concatenate([chip, other_chip], axis=1)
    m, l, acc = attend_first(prompt_q, cont_q, own, *state)
    near_chip, near_other, m, l, acc = tie(near_chip, near_other, m, l, acc)
    near = jnp.concatenate([near_chip, near_other], axis=1)
    l_first, acc_first = l, acc

    over, slabs = jnp.zeros(EXCESS.shape, EXCESS.dtype), []
    for step in (1, 2, 3):
        other = swap(near)
        slabs += [near, other]
        coming = pass_on(near)
        l, acc, over = attend_middle(step, prompt_q, cont_q, near, other, m, l, acc, over)
        near, l, acc, over = tie(coming, l, acc, over)
    mixed = attend_last(meta, prompt_q, cont_q, *slabs, near, m, l, acc, over, l_first, acc_first)
    moved = lax.all_to_all(mixed, "head", split_axis=0, concat_axis=0, tiled=True)
    return lay_out(moved)


def solution(mesh):
    placed = (
        P(("group", "ctx"), "head"),
        P(None, ("group", "ctx"), "head"),
        P(("group", "ctx"), None, "head"),
        P(None, ("group", "ctx"), None, "head"),
        P(("group", "ctx")),
    )
    return jax.shard_map(
        body,
        mesh=mesh,
        in_specs=placed,
        out_specs=(P(("group", "ctx", "head"), None), P(("group", "ctx"), "head", None)),
        check_vma=False,
    )
```
